32 devices in a mesh: groups: 2 (over y), fsdp: 8 (over z, core), band: 2 (over x).
Axes of the slice: x: 2, y: 2, z: 4, core: 2. Of those that a mesh axis runs over, the one named last changes fastest.
Arguments:
- hidden_in: bfloat16 [16, 4, 64, 5632], P(('groups', 'fsdp'), 'band'), parts along dimension 0, may hold values from -6 to 6
- tap_weights: bfloat16 [9, 5632], P(None, 'fsdp'), may hold values from -2 to 2
- tap_bias: bfloat16 [5632], P('fsdp'), may hold values from -3 to 3
- w_out: bfloat16 [2816, 2240], P('fsdp'), may hold values from -0.109375 to 0.109375
- cotangent: bfloat16 [16, 4, 64, 2240], P(('groups', 'fsdp'), 'band'), parts along dimension 0, may hold values from -0.59765625 to 0.59765625
Outputs:
- block_out: bfloat16 [16, 4, 64, 2240], P(('groups', 'fsdp'), 'band'), parts along dimension 0
- d_hidden: bfloat16 [16, 4, 64, 5632], P(('groups', 'fsdp'), 'band'), parts along dimension 0
- d_taps: float32 [18, 5632], P('groups', 'fsdp'), parts along dimension 0
- d_tap_bias: float32 [11264], P(('groups', 'fsdp')), parts along dimension 0
The draws below stay inside these ranges and needn't reach their ends.
There are 2 independent parts, one for each index of `groups`. The reference program is written for one: setup_inputs(seed, part) draws one part's arguments, and reference() takes and returns one part's arrays. A program takes and returns all parts, laid end to end along the dimension named above; an argument that names none is the same for every part. Nothing has to cross between parts.
All inputs are finite; a program needn't handle non-finite values.
Results may differ from the reference program's by a relative error of at most 0.0049.
Values may be sent and summed in bfloat16 or wider, within the bound.
A program may use at most 128 MiB of HBM per device.

```python
import jax
import jax.numpy as jnp
from jax import lax

D = 2240
HID = 2816
CH = 5632
COLS = 64
ROWS = 4
SAMPLES = 8


def shard_levels(own_key, extent, pieces, low, largest):
    def one(axis_at, shards_of):
        draws = jax.random.uniform(jax.random.fold_in(jax.random.fold_in(own_key, 6), axis_at), (shards_of,), jnp.float32, low / len(pieces), largest / len(pieces))
        return jnp.repeat(jnp.exp(draws), extent[axis_at] // shards_of).reshape((-1,) + (1,) * (len(extent) - axis_at - 1))

    level = one(*pieces[0])
    for cut in pieces[1:]:
        level = level * one(*cut)
    return level


def centred(own_key, dims, width, most, cuts=(), held_as=jnp.bfloat16):
    array = jax.random.normal(own_key, dims, jnp.float32) * width
    if len(cuts) > 0:
        array = shard_levels(own_key, dims, cuts, -0.22, 0.18) * array
    return jnp.clip(array, min=-most, max=most).astype(held_as)


def setup_inputs(seed: int = 0, part: int = 0) -> dict:
    keys = jax.random.split(jax.random.key(seed), 6)
    part_keys = jax.random.split(jax.random.fold_in(keys[5], part), 6)
    hidden_in = centred(part_keys[0], (SAMPLES, ROWS, COLS, CH), 1.0, 6.0, ((0, 8), (1, 2)))
    tap_weights = centred(keys[1], (9, CH), 9 ** -0.5, 2.0, ((1, 8),))
    tap_bias = centred(keys[2], (CH,), 0.5, 3.0, ((0, 8),))
    w_out = centred(keys[3], (HID, D), HID ** -0.5, 0.109375, ((0, 8),))
    cotangent = centred(part_keys[4], (SAMPLES, ROWS, COLS, D), 0.1, 0.59765625, ((0, 8), (1, 2)))
    return {"hidden_in": hidden_in, "tap_weights": tap_weights, "tap_bias": tap_bias, "w_out": w_out, "cotangent": cotangent}


def one_image(pair, tap_weights, tap_bias, w_out):
    image, grad_out = pair
    row_count, col_count, channels = image.shape
    hidden_units = channels // 2
    padded = jnp.pad(image, ((1, 1), (1, 1), (0, 0)))
    kernel = tap_weights.astype(jnp.float32)
    offset = tap_bias.astype(jnp.float32)
    summed = jnp.zeros((row_count, col_count, channels), jnp.float32) + offset
    for tap_row in range(3):
        for tap_col in range(3):
            window = padded[tap_row:tap_row + row_count, tap_col:tap_col + col_count, :].astype(jnp.float32)
            summed = summed + kernel[3 * tap_row + tap_col] * window
    values_half = summed[..., :hidden_units]
    gate_half = summed[..., hidden_units:]
    sigmoid_gate = jax.nn.sigmoid(gate_half)
    silu_gate = gate_half * sigmoid_gate
    glu_out = (values_half * silu_gate).astype(jnp.bfloat16)
    flat_glu = glu_out.reshape(row_count * col_count, hidden_units)
    block_out = jnp.dot(flat_glu, w_out, preferred_element_type=jnp.float32).astype(jnp.bfloat16)
    block_out = block_out.reshape(row_count, col_count, -1)
    flat_grad = grad_out.reshape(row_count * col_count, -1)
    d_glu = jnp.dot(flat_grad, w_out.T, preferred_element_type=jnp.float32).reshape(row_count, col_count, hidden_units)
    slope = sigmoid_gate * (1.0 + gate_half * (1.0 - sigmoid_gate))
    d_pre = jnp.concatenate([d_glu * silu_gate, d_glu * values_half * slope], axis=-1).astype(jnp.bfloat16)
    d_pad = jnp.pad(d_pre, ((1, 1), (1, 1), (0, 0))).astype(jnp.float32)
    d_pre_wide = d_pre.astype(jnp.float32)
    d_image = jnp.zeros((row_count, col_count, channels), jnp.float32)
    tap_terms = []
    for tap_row in range(3):
        for tap_col in range(3):
            d_image = d_image + kernel[3 * tap_row + tap_col] * d_pad[2 - tap_row:2 - tap_row + row_count, 2 - tap_col:2 - tap_col + col_count, :]
            window = padded[tap_row:tap_row + row_count, tap_col:tap_col + col_count, :].astype(jnp.float32)
            tap_terms.append(jnp.sum(window * d_pre_wide, axis=(0, 1)))
    return block_out, d_image.astype(jnp.bfloat16), jnp.stack(tap_terms), jnp.sum(d_pre_wide, axis=(0, 1))


def reference(hidden_in, tap_weights, tap_bias, w_out, cotangent):
    def apply_one(pair):
        return one_image(pair, tap_weights, tap_bias, w_out)

    block_out, d_hidden, tap_parts, bias_parts = lax.map(apply_one, (hidden_in, cotangent))
    return block_out, d_hidden, jnp.sum(tap_parts, axis=0), jnp.sum(bias_parts, axis=0)
```

```python
import functools

import jax
import jax.numpy as jnp
from jax import lax
from jax.experimental import pallas as pl
from jax.experimental.pallas import tpu as pltpu
from jax.sharding import PartitionSpec as P

MESH = pl.DeviceIdType.MESH
LANES = 128
PIECE = 32
F32 = jnp.float32
BF16 = jnp.bfloat16


def with_halo(cells, sides, width):
    for axis, dim in sides:
        count = lax.axis_size(axis)
        ends = count - 1
        head = lax.slice_in_dim(cells, 0, width, axis=dim)
        tail = lax.slice_in_dim(cells, cells.shape[dim] - width, cells.shape[dim], axis=dim)
        cells = jnp.concatenate(
            [
                lax.ppermute(tail, axis, [(i, (i + 1) % count) for i in range(ends)]),
                cells,
                lax.ppermute(head, axis, [((i + 1) % count, i) for i in range(ends)]),
            ],
            axis=dim,
        )
    return cells


def general_body(hidden_in, tap_weights, tap_bias, w_out, cotangent):
    kernel_all, offset_all = (
        lax.all_gather(tap_weights, "fsdp", axis=1, tiled=True),
        lax.all_gather(tap_bias, "fsdp", axis=0, tiled=True),
    )
    kernel = kernel_all.astype(jnp.float32)
    offset = offset_all.astype(jnp.float32)
    image_count, row_count, col_count, channels = hidden_in.shape
    hidden_units = channels // 2
    token_count = image_count * row_count * col_count
    extended = with_halo(hidden_in, (("band", 1),), 1)
    padded = jnp.pad(extended, ((0, 0), (0, 0), (1, 1), (0, 0)))
    summed = jnp.zeros((image_count, row_count, col_count, channels), jnp.float32) + offset
    for tap_row in range(3):
        for tap_col in range(3):
            window = padded[:, tap_row : tap_row + row_count, tap_col : tap_col + col_count, :]
            summed = summed + kernel[3 * tap_row + tap_col] * window
    values_half = summed[..., :hidden_units]
    gate_half = summed[..., hidden_units:]
    sigmoid_gate = jax.nn.sigmoid(gate_half)
    silu_gate = gate_half * sigmoid_gate
    glu_flat = (values_half * silu_gate).astype(jnp.bfloat16).reshape(token_count, hidden_units)
    grad_flat = cotangent.reshape(token_count, cotangent.shape[3])
    features = grad_flat.shape[1]
    piece = lax.all_gather(w_out, "fsdp", axis=0, tiled=True)
    out_sum = jnp.dot(glu_flat, piece, preferred_element_type=jnp.float32)
    d_glu = lax.dot_general(
        grad_flat, piece, (((1,), (1,)), ((), ())), preferred_element_type=jnp.float32
    )
    block_out = out_sum.astype(jnp.bfloat16).reshape(image_count, row_count, col_count, features)
    d_glu = d_glu.reshape(image_count, row_count, col_count, hidden_units)
    slope = sigmoid_gate * (1.0 + gate_half * (1.0 - sigmoid_gate))
    d_pre = jnp.concatenate([d_glu * silu_gate, d_glu * values_half * slope], axis=-1).astype(
        jnp.bfloat16
    )
    d_extended = with_halo(d_pre, (("band", 1),), 1)
    d_pad = jnp.pad(d_extended, ((0, 0), (0, 0), (1, 1), (0, 0)))
    d_image = jnp.zeros((image_count, row_count, col_count, channels), jnp.float32)
    tap_terms = []
    for tap_row in range(3):
        for tap_col in range(3):
            d_window = d_pad[
                :, 2 - tap_row : 2 - tap_row + row_count, 2 - tap_col : 2 - tap_col + col_count, :
            ]
            d_image = d_image + kernel[3 * tap_row + tap_col] * d_window
            window = padded[:, tap_row : tap_row + row_count, tap_col : tap_col + col_count, :]
            tap_terms.append(
                jnp.einsum("srck,srck->k", window, d_pre, preferred_element_type=jnp.float32)
            )
    d_hidden = d_image.astype(jnp.bfloat16)
    tap_grad = jnp.stack(tap_terms)
    bias_grad = jnp.sum(d_pre.astype(jnp.float32), axis=(0, 1, 2))
    tap_grad, bias_grad = lax.psum((tap_grad, bias_grad), "band")
    tap_share, bias_share = (
        lax.psum_scatter(tap_grad, "fsdp", scatter_dimension=1, tiled=True),
        lax.psum_scatter(bias_grad, "fsdp", scatter_dimension=0, tiled=True),
    )
    return (block_out, d_hidden, tap_share, bias_share)


def halo_groups(blocks):
    first = min(2, blocks)
    second = min(3, blocks - first)
    sizes = [n for n in (first, second, blocks - first - second) if n > 0]
    starts = [sum(sizes[:i]) for i in range(len(sizes))]
    return list(zip(starts, sizes))


def unit_kernel(
    hid, taps, w, cot,
    out, dhid, tgrad,
    W, C, H, HH, T, TF, GLU, D, DH, DHS, G, GS, R, PS, PR,
    bar_dummy,
    s_own, s_cot, s_d2d_s, s_d2d_r, s_up, s_dn, s_zr, s_ys, s_yr,
    s_hl, s_hs, s_hr, s_hxs, s_hxr,
    s_ts, s_tr, s_ds, s_dr, s_ol, s_os, s_or, s_gs, s_gr, s_ps, s_pr,
):
    y = lax.axis_index("groups")
    f = lax.axis_index("fsdp")
    x = lax.axis_index("band")
    z, c = f // 2, f % 2
    sib = z * 2 + (1 - c)
    nz = lax.axis_size("fsdp") // 2
    shard, features = w.shape
    half = W.shape[0]
    plane = 2 * shard
    hidden_units = 2 * half
    blocks = half // LANES
    steps = half // (2 * PIECE)
    own_steps = steps // 2
    s = jnp.where(c == 0, z, nz - 1 - z)
    up = jnp.where(c == 0, f + 2, f - 2)
    down = jnp.where(c == 0, f - 2, f + 2)
    source = s < 2
    groups = halo_groups(blocks)

    def ascending(core, zz):
        pos = jnp.where(core == 0, zz, nz - 1 - zz)
        return (core == 1) != (pos == 0)

    asc = ascending(c, z)

    def block_of(j):
        return jnp.where(asc, j, blocks - 1 - j)

    def al(v, m):
        return pl.multiple_of(v, m)

    barrier = pltpu.get_barrier_semaphore()
    count = 0
    for df in range(2 * nz):
        for dx in range(2):
            if df == 0 and dx == 0:
                continue
            pl.semaphore_signal(
                barrier, inc=1, device_id=(y, lax.rem(f + df, 2 * nz), lax.rem(x + dx, 2)),
                device_id_type=MESH,
            )
            count += 1
    pl.semaphore_signal(barrier, inc=1, device_id=(1 - y, f, x), device_id_type=MESH)
    pl.semaphore_wait(barrier, count + 1)

    my_base = (z % 2) * plane

    def own_copy():
        return pltpu.make_async_copy(w, W.at[pl.ds(al(my_base + c * shard, 16), shard)], s_own)

    def d2d(k):
        at = jnp.where(c == 1, shard - PIECE * (k + 1), PIECE * k)
        at = al(at, PIECE)
        return pltpu.make_async_remote_copy(
            w.at[pl.ds(at, PIECE)],
            W.at[pl.ds(al(my_base + c * shard + at, PIECE), PIECE)],
            s_d2d_s.at[k], s_d2d_r.at[k], device_id=(y, sib, x), device_id_type=MESH,
        )

    def rows_of(u, yy):
        return al(jnp.where(c == 0, half - 2 * PIECE * (u + 1), 2 * PIECE * u) + PIECE * yy, PIECE)

    def z_up(u):
        r = W.at[pl.ds(rows_of(u, y), PIECE)]
        return pltpu.make_async_remote_copy(
            r, r, s_up.at[u], s_zr.at[u], device_id=(y, up, x), device_id_type=MESH
        )

    def z_down(u):
        r = W.at[pl.ds(rows_of(u, y), PIECE)]
        return pltpu.make_async_remote_copy(
            r, r, s_dn.at[u], s_zr.at[u], device_id=(y, down, x), device_id_type=MESH
        )

    def y_copy(u, yy):
        r = W.at[pl.ds(rows_of(u, yy), PIECE)]
        return pltpu.make_async_remote_copy(
            r, r, s_ys.at[u], s_yr.at[u], device_id=(1 - y, f, x), device_id_type=MESH
        )

    def lane_at(a, g):
        st, n = groups[g]
        return jnp.where(a, LANES * st, LANES * (blocks - st - n))

    def hid_local(g, k):
        n = groups[g][1] * LANES
        at = lane_at(asc, g)
        return pltpu.make_async_copy(
            hid.at[0, :, :, pl.ds(al(k * hidden_units + c * half + at, LANES), n)],
            H.at[k, c, :, :, pl.ds(al(at, LANES), n)], s_hl.at[g, k],
        )

    def hid_sib(g, k, sending):
        n = groups[g][1] * LANES
        core = 1 - c if sending else c
        at = lane_at(ascending(core, z), g)
        return pltpu.make_async_remote_copy(
            hid.at[0, :, :, pl.ds(al(k * hidden_units + core * half + at, LANES), n)],
            H.at[k, c if sending else 1 - c, :, :, pl.ds(al(at, LANES), n)],
            s_hs.at[g, k], s_hr.at[g, k], device_id=(y, sib, x), device_id_type=MESH,
        )

    def hid_x_send(core, g, k):
        n = groups[g][1] * LANES
        at = lane_at(ascending(core, z), g)
        return pltpu.make_async_remote_copy(
            hid.at[0, 1 - x, :, pl.ds(al(k * hidden_units + core * half + at, LANES), n)],
            HH.at[k, c, :, pl.ds(al(at, LANES), n)],
            s_hxs.at[core, g, k], s_hxr.at[c, g, k],
            device_id=(y, 2 * z + core, 1 - x), device_id_type=MESH,
        )

    def hid_x_recv(img, g, k):
        n = groups[g][1] * LANES
        r = HH.at[k, img, :, pl.ds(al(lane_at(asc, g), LANES), n)]
        return pltpu.make_async_remote_copy(
            r, r, s_hxs.at[0, g, k], s_hxr.at[img, g, k],
            device_id=(y, f, 1 - x), device_id_type=MESH,
        )

    cot_local = pltpu.make_async_copy(cot, C.at[c], s_cot.at[0])

    def cot_sib(img):
        return pltpu.make_async_remote_copy(
            cot, C.at[img], s_cot.at[1], s_cot.at[2], device_id=(y, sib, x), device_id_type=MESH
        )

    tap_core = z % 2
    tap_slot = 2 * (z // 2) + c

    def tap_send(zz):
        return pltpu.make_async_remote_copy(
            taps, T.at[tap_slot], s_ts.at[zz], s_tr.at[tap_slot],
            device_id=(y, 2 * zz + tap_core, x), device_id_type=MESH,
        )

    def tap_local(slot):
        return pltpu.make_async_copy(taps, T.at[slot], s_tr.at[slot])

    def d_halo(b, row):
        return pltpu.make_async_remote_copy(
            D.at[b, row], DH.at[b], s_ds.at[b], s_dr.at[b],
            device_id=(y, f, 1 - x), device_id_type=MESH,
        )

    is_self = tap_core == c
    for zz in range(4):
        @pl.when(jnp.logical_or(jnp.logical_not(is_self), z != zz))
        def _():
            tap_send(zz).start()

    @pl.when(is_self)
    def _():
        tap_local(tap_slot).start()

    @pl.when(jnp.logical_not(source))
    def _():
        for k in range(shard // PIECE):
            d2d(k).start()

    @pl.when(source)
    def _():
        own_copy().start()

    for g in range(len(groups)):
        for k in range(2):
            for core in range(2):
                hid_x_send(core, g, k).start()
            hid_local(g, k).start()
            hid_sib(g, k, True).start()
        if g == 0:
            cot_local.start()
            cot_sib(c).start()

    split = (shard // PIECE + 1) // 2
    n_d2d = shard // PIECE

    @pl.when(source)
    def _():
        own_copy().wait()

        @pl.when(s == 1)
        def _():
            for u in range(own_steps - 1, split - 1, -1):
                z_down(u).start()

        first = jnp.where(s == 1, 0, own_steps)
        for i in range(own_steps):
            for m in (2 * i, 2 * i + 1):
                if m < n_d2d:
                    at = al(jnp.where(c == 0, plane - PIECE * (m + 1), PIECE * m), PIECE)
                    r = W.at[pl.ds(al(my_base + at, PIECE), PIECE)]
                    pltpu.make_async_remote_copy(
                        r, r, s_d2d_s.at[m], s_d2d_r.at[m],
                        device_id=(y, sib, x), device_id_type=MESH,
                    ).wait_recv()
            z_up(first + i).start()

        @pl.when(s == 1)
        def _():
            for u in range(split - 1, -1, -1):
                z_down(u).start()

    for slot in range(4):
        tap_local(slot).wait()
    for k in range(2):
        TF[k] = jnp.concatenate(
            [T[2 * k].astype(F32), T[2 * k + 1].astype(F32)], axis=1
        )
    cot_local.wait()
    cot_sib(1 - c).wait_recv()

    col = lax.broadcasted_iota(jnp.int32, (H.shape[3], LANES), 0)
    cols = H.shape[3]

    def before(a):
        return jnp.where(col == 0, 0.0, pltpu.roll(a, 1, 0))

    def after(a):
        return jnp.where(col == cols - 1, 0.0, pltpu.roll(a, cols - 1, 0))

    def needed(u):
        return jnp.logical_or(
            s >= 2,
            jnp.logical_or(
                jnp.logical_and(s == 0, u < own_steps), jnp.logical_and(s == 1, u >= own_steps)
            ),
        )

    def u_of(i):
        return jnp.where(s == 0, steps - 1 - i, i)

    def take(j):
        for h in range(2):
            u = u_of(2 * j + h)

            @pl.when(needed(u))
            def _():
                z_up(u).wait_recv()

                @pl.when(jnp.logical_or(s == 1, s == 2))
                def _():
                    z_up(u).start()

                y_copy(u, y).start()

    def halo_in(g):
        for k in range(2):
            hid_local(g, k).wait()
            hid_sib(g, k, False).wait_recv()
            for img in range(2):
                hid_x_recv(img, g, k).wait_recv()

    def stage_a(j):
        b = block_of(j)
        lane = pl.ds(al(b * LANES, LANES), LANES)
        for h in range(2):
            u = u_of(2 * j + h)

            @pl.when(needed(u))
            def _():
                y_copy(u, 1 - y).wait_recv()

        wb = W[lane, :]
        ext = {}
        tf = [TF[k, :, lane] for k in range(2)]
        sums = [[None] * 10, [None] * 10]
        for img in range(2):
            dg = lax.dot_general(
                C[img], wb, (((1,), (1,)), ((), ())), preferred_element_type=F32
            )
            pre = [[], []]
            rows = [None, None]
            for k in range(2):
                hal = HH[k, img, :, lane].astype(F32)
                rows[k] = [
                    jnp.where(x == 1, hal, 0.0),
                    H[k, img, 0, :, lane].astype(F32),
                    H[k, img, 1, :, lane].astype(F32),
                    jnp.where(x == 0, hal, 0.0),
                ]
                for r in range(2):
                    a = [
                        sum(tf[k][3 * i + jj : 3 * i + jj + 1] * rows[k][r + i] for i in range(3))
                        for jj in range(3)
                    ]
                    pre[k].append(before(a[0]) + (a[1] + tf[k][9:10]) + after(a[2]))
            for r in range(2):
                v, gt = pre[0][r], pre[1][r]
                sg = jax.nn.sigmoid(gt)
                si = gt * sg
                at = img * 2 * cols + r * cols
                GLU[at : at + cols, lane] = (v * si).astype(BF16)
                d = dg[r * cols : (r + 1) * cols]
                dv = (d * si).astype(BF16)
                dq = (d * v * (sg * (1.0 + gt * (1.0 - sg)))).astype(BF16)
                D[b, r, 0, img] = dv
                D[b, r, 1, img] = dq
                for k, dd in ((0, dv), (1, dq)):
                    dd = dd.astype(F32)
                    shifted = (after(dd), dd, before(dd))
                    for i in range(3):
                        for jj in range(3):
                            t = rows[k][r + i] * shifted[jj]
                            n = 3 * i + jj
                            sums[k][n] = t if sums[k][n] is None else sums[k][n] + t
                    sums[k][9] = dd if sums[k][9] is None else sums[k][9] + dd
        d_halo(b, 1 - x).start()
        for k in range(2):
            for n in range(10):
                G[k, n : n + 1, lane] = jnp.sum(sums[k][n], axis=0, keepdims=True)

    def out_lanes(b, k):
        return pl.ds(al(k * hidden_units + c * half + b * LANES, LANES), LANES)

    def o_local(b, k):
        lane = pl.ds(al(b * LANES, LANES), LANES)
        return pltpu.make_async_copy(
            DHS.at[k, c, :, :, lane], dhid.at[0, :, :, out_lanes(b, k)], s_ol.at[b, k]
        )

    def o_sib(b, k):
        lane = pl.ds(al(b * LANES, LANES), LANES)
        return pltpu.make_async_remote_copy(
            DHS.at[k, 1 - c, :, :, lane], dhid.at[0, :, :, out_lanes(b, k)],
            s_os.at[b, k], s_or.at[b, k], device_id=(y, sib, x), device_id_type=MESH,
        )

    def o_sib_in(b, k):
        lane = pl.ds(al(b * LANES, LANES), LANES)
        return pltpu.make_async_remote_copy(
            DHS.at[k, c, :, :, lane],
            dhid.at[0, :, :, pl.ds(al(k * hidden_units + (1 - c) * half + b * LANES, LANES), LANES)],
            s_os.at[b, k], s_or.at[b, k], device_id=(y, sib, x), device_id_type=MESH,
        )

    def stage_b(j):
        b = block_of(j)
        lane = pl.ds(al(b * LANES, LANES), LANES)
        d_halo(b, 1 - x).wait_recv()
        for k in range(2):
            tf = TF[k, :, lane]
            for img in range(2):
                hal = DH[b, k, img].astype(F32)
                rows = [
                    jnp.where(x == 1, hal, 0.0),
                    D[b, 0, k, img].astype(F32),
                    D[b, 1, k, img].astype(F32),
                    jnp.where(x == 0, hal, 0.0),
                ]
                for r in range(2):
                    a = [
                        sum(tf[3 * i + jj : 3 * i + jj + 1] * rows[r + 2 - i] for i in range(3))
                        for jj in range(3)
                    ]
                    DHS[k, img, r, :, lane] = (after(a[0]) + a[1] + before(a[2])).astype(BF16)
            o_local(b, k).start()
            o_sib(b, k).start()

    take(0)

    @pl.loop(0, blocks)
    def _(j):
        for g in range(len(groups)):
            @pl.when(j == groups[g][0])
            def _():
                halo_in(g)

        @pl.when(j < blocks - 1)
        def _():
            take(j + 1)

        stage_a(j)

        @pl.when(j >= 2)
        def _():
            stage_b(j - 2)

    for k in range(2):
        GS[2 * k] = G[k, :, 0:plane]
        GS[2 * k + 1] = G[k, :, plane:]

    my_slot = 2 * z + x

    def g_dev(n, xx):
        return 2 * (2 * (n // 2) + c) + (n % 2)

    def g_send(n, xx):
        return pltpu.make_async_remote_copy(
            GS.at[n], R.at[my_slot], s_gs.at[n, xx], s_gr.at[my_slot],
            device_id=(y, g_dev(n, xx), xx), device_id_type=MESH,
        )

    def g_self(n, xx):
        return jnp.logical_and(g_dev(n, xx) == f, x == xx)

    for n in range(4):
        for xx in range(2):
            @pl.when(g_self(n, xx))
            def _():
                pltpu.make_async_copy(GS.at[n], R.at[my_slot], s_gr.at[my_slot]).start()

            @pl.when(jnp.logical_not(g_self(n, xx)))
            def _():
                g_send(n, xx).start()

    tokens = 2 * cols
    part = []
    n_at = 0
    while n_at < features:
        part.append((n_at, min(512, features - n_at)))
        n_at += 512

    def product(img, at, n):
        g = GLU[pl.ds(al(img * tokens, tokens), tokens), :]
        return jnp.dot(g, W[:, at : at + n], preferred_element_type=F32)

    for at, n in part:
        PS[:, at : at + n] = product(1 - c, at, n).astype(BF16)
    p_copy = pltpu.make_async_remote_copy(
        PS, PR, s_ps, s_pr, device_id=(y, sib, x), device_id_type=MESH
    )
    p_copy.start()
    stage_b(blocks - 2)
    stage_b(blocks - 1)
    mine = [product(c, at, n) for at, n in part]
    p_copy.wait_recv()
    for (at, n), m in zip(part, mine):
        out[:, at : at + n] = (m + PR[:, at : at + n].astype(F32)).astype(BF16)

    for slot in range(8):
        pltpu.make_async_copy(GS.at[0], R.at[slot], s_gr.at[slot]).wait()
    total = R[0]
    for slot in range(1, 8):
        total = total + R[slot]
    tgrad[...] = total

    for n in range(4):
        for xx in range(2):
            @pl.when(jnp.logical_not(g_self(n, xx)))
            def _():
                g_send(n, xx).wait_send()
    p_copy.wait_send()
    for zz in range(4):
        @pl.when(jnp.logical_or(jnp.logical_not(is_self), z != zz))
        def _():
            tap_send(zz).wait_send()

    @pl.when(jnp.logical_not(source))
    def _():
        for k in range(n_d2d):
            d2d(k).wait_send()

    cot_sib(c).wait_send()
    for g in range(len(groups)):
        for k in range(2):
            for core in range(2):
                hid_x_send(core, g, k).wait_send()
            hid_sib(g, k, True).wait_send()

    @pl.loop(0, steps)
    def _(u):
        @pl.when(jnp.logical_or(s == 1, jnp.logical_or(s == 2, jnp.logical_and(s == 0, u >= own_steps))))
        def _():
            z_up(u).wait_send()

        @pl.when(jnp.logical_and(s == 1, u < own_steps))
        def _():
            z_down(u).wait_send()

        @pl.when(needed(u))
        def _():
            y_copy(u, y).wait_send()

    @pl.loop(0, blocks)
    def _(b):
        d_halo(b, 1 - x).wait_send()
        for k in range(2):
            o_local(b, k).wait()
            o_sib(b, k).wait_send()
            o_sib_in(b, k).wait_recv()


def fused_body(hidden_in, tap_weights, tap_bias, w_out, cotangent):
    _, rows, cols, channels = hidden_in.shape
    shard, features = w_out.shape
    own_channels = tap_weights.shape[1]
    half = channels // 4
    blocks = half // LANES
    tokens = rows * cols
    taps = jnp.concatenate(
        [tap_weights, tap_bias[None], jnp.zeros((6, own_channels), BF16)], axis=0
    )
    steps = half // (2 * PIECE)
    n_groups = len(halo_groups(blocks))
    dma = pltpu.SemaphoreType.DMA
    flops = 2 * 2 * 2 * tokens * half * features
    out, d_hidden, tgrad = pl.pallas_call(
        unit_kernel,
        out_shape=(
            jax.ShapeDtypeStruct((tokens, features), BF16),
            jax.ShapeDtypeStruct(hidden_in.shape, BF16),
            jax.ShapeDtypeStruct((16, own_channels), F32),
        ),
        in_specs=[
            pl.BlockSpec(memory_space=pl.ANY),
            pl.BlockSpec(memory_space=pltpu.VMEM),
            pl.BlockSpec(memory_space=pl.ANY),
            pl.BlockSpec(memory_space=pl.ANY),
        ],
        out_specs=(
            pl.BlockSpec(memory_space=pltpu.VMEM),
            pl.BlockSpec(memory_space=pl.ANY),
            pl.BlockSpec(memory_space=pltpu.VMEM),
        ),
        scratch_shapes=[
            pltpu.VMEM((half, features), BF16),
            pltpu.VMEM((2, tokens, features), BF16),
            pltpu.VMEM((2, 2, rows, cols, half), BF16),
            pltpu.VMEM((2, 2, cols, half), BF16),
            pltpu.VMEM((4, 16, own_channels), BF16),
            pltpu.VMEM((2, 16, half), F32),
            pltpu.VMEM((2 * tokens, half), BF16),
            pltpu.VMEM((blocks, rows, 2, 2, cols, LANES), BF16),
            pltpu.VMEM((blocks, 2, 2, cols, LANES), BF16),
            pltpu.VMEM((2, 2, rows, cols, half), BF16),
            pltpu.VMEM((2, 16, half), F32),
            pltpu.VMEM((4, 16, own_channels), F32),
            pltpu.VMEM((8, 16, own_channels), F32),
            pltpu.VMEM((tokens, features), BF16),
            pltpu.VMEM((tokens, features), BF16),
            pltpu.SemaphoreType.REGULAR,
            dma, dma((3,)), dma((shard // PIECE,)), dma((shard // PIECE,)),
            dma((steps,)), dma((steps // 2,)), dma((steps,)), dma((steps,)), dma((steps,)),
            dma((n_groups, 2)), dma((n_groups, 2)), dma((n_groups, 2)),
            dma((2, n_groups, 2)), dma((2, n_groups, 2)),
            dma((4,)), dma((4,)), dma((blocks,)), dma((blocks,)),
            dma((blocks, 2)), dma((blocks, 2)), dma((blocks, 2)),
            dma((4, 2)), dma((8,)), dma, dma,
        ],
        compiler_params=pltpu.CompilerParams(
            collective_id=0, has_side_effects=True, vmem_limit_bytes=56 * 1024 * 1024
        ),
        cost_estimate=pl.CostEstimate(flops=flops, bytes_accessed=8 << 20, transcendentals=0),
    )(hidden_in, taps, w_out, cotangent.reshape(tokens, features))
    return (
        out.reshape(cotangent.shape), d_hidden, tgrad[:9], tgrad[9],
    )


def fits(mesh, hidden_in, tap_weights, tap_bias, w_out, cotangent):
    if (mesh.shape["groups"], mesh.shape["fsdp"], mesh.shape["band"]) != (2, 8, 2):
        return False
    images, rows, cols, channels = hidden_in.shape
    return (
        images == 1
        and rows == 2
        and cols % 16 == 0
        and (channels // 4) % (2 * LANES) == LANES
        and w_out.shape[0] % PIECE == 0
        and (w_out.shape[0] // PIECE) % 2 == 1
        and 4 * w_out.shape[0] == channels // 4
        and 8 * tap_weights.shape[1] == channels
    )


def body(mesh, *args):
    if fits(mesh, *args):
        return fused_body(*args)
    return general_body(*args)


def solution(mesh):
    placed = (
        P(("groups", "fsdp"), "band", None, None),
        P(None, "fsdp"),
        P("fsdp"),
        P("fsdp", None),
        P(("groups", "fsdp"), "band", None, None),
    )
    return jax.shard_map(
        functools.partial(body, mesh),
        mesh=mesh,
        in_specs=placed,
        out_specs=(
            P(("groups", "fsdp"), "band", None, None),
            P(("groups", "fsdp"), "band", None, None),
            P("groups", "fsdp"),
            P(("groups", "fsdp")),
        ),
        check_vma=False,
    )
```

```python
import functools

import jax
import jax.numpy as jnp
from jax import lax
from jax.experimental import pallas as pl
from jax.experimental.pallas import tpu as pltpu
from jax.sharding import PartitionSpec as P

MESH = pl.DeviceIdType.MESH
LANES = 128
PIECE = 32
AHEAD = 4
F32 = jnp.float32
BF16 = jnp.bfloat16


def with_halo(cells, sides, width):
    for axis, dim in sides:
        count = lax.axis_size(axis)
        ends = count - 1
        head = lax.slice_in_dim(cells, 0, width, axis=dim)
        tail = lax.slice_in_dim(cells, cells.shape[dim] - width, cells.shape[dim], axis=dim)
        cells = jnp.concatenate(
            [
                lax.ppermute(tail, axis, [(i, (i + 1) % count) for i in range(ends)]),
                cells,
                lax.ppermute(head, axis, [((i + 1) % count, i) for i in range(ends)]),
            ],
            axis=dim,
        )
    return cells


def general_body(hidden_in, tap_weights, tap_bias, w_out, cotangent):
    kernel_all, offset_all = (
        lax.all_gather(tap_weights, "fsdp", axis=1, tiled=True),
        lax.all_gather(tap_bias, "fsdp", axis=0, tiled=True),
    )
    kernel = kernel_all.astype(jnp.float32)
    offset = offset_all.astype(jnp.float32)
    image_count, row_count, col_count, channels = hidden_in.shape
    hidden_units = channels // 2
    token_count = image_count * row_count * col_count
    extended = with_halo(hidden_in, (("band", 1),), 1)
    padded = jnp.pad(extended, ((0, 0), (0, 0), (1, 1), (0, 0)))
    summed = jnp.zeros((image_count, row_count, col_count, channels), jnp.float32) + offset
    for tap_row in range(3):
        for tap_col in range(3):
            window = padded[:, tap_row : tap_row + row_count, tap_col : tap_col + col_count, :]
            summed = summed + kernel[3 * tap_row + tap_col] * window
    values_half = summed[..., :hidden_units]
    gate_half = summed[..., hidden_units:]
    sigmoid_gate = jax.nn.sigmoid(gate_half)
    silu_gate = gate_half * sigmoid_gate
    glu_flat = (values_half * silu_gate).astype(jnp.bfloat16).reshape(token_count, hidden_units)
    grad_flat = cotangent.reshape(token_count, cotangent.shape[3])
    features = grad_flat.shape[1]
    piece = lax.all_gather(w_out, "fsdp", axis=0, tiled=True)
    out_sum = jnp.dot(glu_flat, piece, preferred_element_type=jnp.float32)
    d_glu = lax.dot_general(
        grad_flat, piece, (((1,), (1,)), ((), ())), preferred_element_type=jnp.float32
    )
    block_out = out_sum.astype(jnp.bfloat16).reshape(image_count, row_count, col_count, features)
    d_glu = d_glu.reshape(image_count, row_count, col_count, hidden_units)
    slope = sigmoid_gate * (1.0 + gate_half * (1.0 - sigmoid_gate))
    d_pre = jnp.concatenate([d_glu * silu_gate, d_glu * values_half * slope], axis=-1).astype(
        jnp.bfloat16
    )
    d_extended = with_halo(d_pre, (("band", 1),), 1)
    d_pad = jnp.pad(d_extended, ((0, 0), (0, 0), (1, 1), (0, 0)))
    d_image = jnp.zeros((image_count, row_count, col_count, channels), jnp.float32)
    tap_terms = []
    for tap_row in range(3):
        for tap_col in range(3):
            d_window = d_pad[
                :, 2 - tap_row : 2 - tap_row + row_count, 2 - tap_col : 2 - tap_col + col_count, :
            ]
            d_image = d_image + kernel[3 * tap_row + tap_col] * d_window
            window = padded[:, tap_row : tap_row + row_count, tap_col : tap_col + col_count, :]
            tap_terms.append(
                jnp.einsum("srck,srck->k", window, d_pre, preferred_element_type=jnp.float32)
            )
    d_hidden = d_image.astype(jnp.bfloat16)
    tap_grad = jnp.stack(tap_terms)
    bias_grad = jnp.sum(d_pre.astype(jnp.float32), axis=(0, 1, 2))
    tap_grad, bias_grad = lax.psum((tap_grad, bias_grad), "band")
    tap_share, bias_share = (
        lax.psum_scatter(tap_grad, "fsdp", scatter_dimension=1, tiled=True),
        lax.psum_scatter(bias_grad, "fsdp", scatter_dimension=0, tiled=True),
    )
    return (block_out, d_hidden, tap_share, bias_share)


def halo_groups(blocks):
    first = min(2, blocks)
    second = min(3, blocks - first)
    sizes = [n for n in (first, second, blocks - first - second) if n > 0]
    starts = [sum(sizes[:i]) for i in range(len(sizes))]
    return list(zip(starts, sizes))


def unit_kernel(
    hid, tap_in, bias_in, w, cot,
    out, dhid, tgrad, bgrad,
    W, C, H, HH, T, TF, GLU, D, DH, DHS, G, GS, R, PS, PR,
    taps,
    s_own, s_cot, s_d2d_s, s_d2d_r, s_up, s_dn, s_zr, s_ys, s_yr,
    s_hl, s_hs, s_hr, s_hxs, s_hxr,
    s_ts, s_tr, s_ds, s_dr, s_ol, s_os, s_or, s_gs, s_gr, s_ps, s_pr,
):
    y = lax.axis_index("groups")
    f = lax.axis_index("fsdp")
    x = lax.axis_index("band")
    z, c = f // 2, f % 2
    sib = z * 2 + (1 - c)
    nz = lax.axis_size("fsdp") // 2
    shard, features = w.shape
    half = W.shape[0]
    plane = 2 * shard
    hidden_units = 2 * half
    blocks = half // LANES
    steps = half // (2 * PIECE)
    own_steps = steps // 2
    s = jnp.where(c == 0, z, nz - 1 - z)
    up = jnp.where(c == 0, f + 2, f - 2)
    down = jnp.where(c == 0, f - 2, f + 2)
    source = s < 2
    groups = halo_groups(blocks)

    def ascending(core, zz):
        pos = jnp.where(core == 0, zz, nz - 1 - zz)
        return (core == 1) != (pos == 0)

    asc = ascending(c, z)

    def block_of(j):
        return jnp.where(asc, j, blocks - 1 - j)

    def al(v, m):
        return pl.multiple_of(v, m)

    taps[...] = jnp.zeros_like(taps)
    taps[0:9] = tap_in[...].astype(F32)
    taps[9:10] = bias_in[...].astype(F32)

    barrier = pltpu.get_barrier_semaphore()
    count = 0
    for df in range(2 * nz):
        for dx in range(2):
            if df == 0 and dx == 0:
                continue
            pl.semaphore_signal(
                barrier, inc=1, device_id=(y, lax.rem(f + df, 2 * nz), lax.rem(x + dx, 2)),
                device_id_type=MESH,
            )
            count += 1
    pl.semaphore_signal(barrier, inc=1, device_id=(1 - y, f, x), device_id_type=MESH)
    pl.semaphore_wait(barrier, count + 1)

    my_base = (z % 2) * plane

    def own_copy():
        return pltpu.make_async_copy(w, W.at[pl.ds(al(my_base + c * shard, 16), shard)], s_own)

    def d2d(k):
        at = jnp.where(c == 1, shard - PIECE * (k + 1), PIECE * k)
        at = al(at, PIECE)
        return pltpu.make_async_remote_copy(
            w.at[pl.ds(at, PIECE)],
            W.at[pl.ds(al(my_base + c * shard + at, PIECE), PIECE)],
            s_d2d_s.at[k], s_d2d_r.at[k], device_id=(y, sib, x), device_id_type=MESH,
        )

    def rows_of(u, yy):
        return al(jnp.where(c == 0, half - 2 * PIECE * (u + 1), 2 * PIECE * u) + PIECE * yy, PIECE)

    def z_up(u):
        r = W.at[pl.ds(rows_of(u, y), PIECE)]
        return pltpu.make_async_remote_copy(
            r, r, s_up.at[u], s_zr.at[u], device_id=(y, up, x), device_id_type=MESH
        )

    def z_down(u):
        r = W.at[pl.ds(rows_of(u, y), PIECE)]
        return pltpu.make_async_remote_copy(
            r, r, s_dn.at[u], s_zr.at[u], device_id=(y, down, x), device_id_type=MESH
        )

    def y_copy(u, yy):
        r = W.at[pl.ds(rows_of(u, yy), PIECE)]
        return pltpu.make_async_remote_copy(
            r, r, s_ys.at[u], s_yr.at[u], device_id=(1 - y, f, x), device_id_type=MESH
        )

    def lane_at(a, g):
        st, n = groups[g]
        return jnp.where(a, LANES * st, LANES * (blocks - st - n))

    def hid_local(g, k):
        n = groups[g][1] * LANES
        at = lane_at(asc, g)
        return pltpu.make_async_copy(
            hid.at[0, :, :, pl.ds(al(k * hidden_units + c * half + at, LANES), n)],
            H.at[k, c, :, :, pl.ds(al(at, LANES), n)], s_hl.at[g, k],
        )

    def hid_sib(g, k, sending):
        n = groups[g][1] * LANES
        core = 1 - c if sending else c
        at = lane_at(ascending(core, z), g)
        return pltpu.make_async_remote_copy(
            hid.at[0, :, :, pl.ds(al(k * hidden_units + core * half + at, LANES), n)],
            H.at[k, c if sending else 1 - c, :, :, pl.ds(al(at, LANES), n)],
            s_hs.at[g, k], s_hr.at[g, k], device_id=(y, sib, x), device_id_type=MESH,
        )

    def hid_x_send(core, g, k):
        n = groups[g][1] * LANES
        at = lane_at(ascending(core, z), g)
        return pltpu.make_async_remote_copy(
            hid.at[0, 1 - x, :, pl.ds(al(k * hidden_units + core * half + at, LANES), n)],
            HH.at[k, c, :, pl.ds(al(at, LANES), n)],
            s_hxs.at[core, g, k], s_hxr.at[c, g, k],
            device_id=(y, 2 * z + core, 1 - x), device_id_type=MESH,
        )

    def hid_x_recv(img, g, k):
        n = groups[g][1] * LANES
        r = HH.at[k, img, :, pl.ds(al(lane_at(asc, g), LANES), n)]
        return pltpu.make_async_remote_copy(
            r, r, s_hxs.at[0, g, k], s_hxr.at[img, g, k],
            device_id=(y, f, 1 - x), device_id_type=MESH,
        )

    cot_local = pltpu.make_async_copy(cot, C.at[c], s_cot.at[0])

    def cot_sib(img):
        return pltpu.make_async_remote_copy(
            cot, C.at[img], s_cot.at[1], s_cot.at[2], device_id=(y, sib, x), device_id_type=MESH
        )

    tap_core = z % 2
    tap_slot = 2 * (z // 2) + c

    def tap_send(zz):
        return pltpu.make_async_remote_copy(
            taps, T.at[tap_slot], s_ts.at[zz], s_tr.at[tap_slot],
            device_id=(y, 2 * zz + tap_core, x), device_id_type=MESH,
        )

    def tap_local(slot):
        return pltpu.make_async_copy(taps, T.at[slot], s_tr.at[slot])

    def d_halo(b, row):
        return pltpu.make_async_remote_copy(
            D.at[b, row], DH.at[b], s_ds.at[b], s_dr.at[b],
            device_id=(y, f, 1 - x), device_id_type=MESH,
        )

    is_self = tap_core == c
    for zz in range(4):
        @pl.when(jnp.logical_or(jnp.logical_not(is_self), z != zz))
        def _():
            tap_send(zz).start()

    @pl.when(is_self)
    def _():
        tap_local(tap_slot).start()

    @pl.when(jnp.logical_not(source))
    def _():
        for k in range(shard // PIECE):
            d2d(k).start()

    @pl.when(source)
    def _():
        own_copy().start()

    for g in range(len(groups)):
        for k in range(2):
            for core in range(2):
                hid_x_send(core, g, k).start()
            hid_local(g, k).start()
            hid_sib(g, k, True).start()
        if g == 0:
            cot_local.start()
            cot_sib(c).start()

    split = (shard // PIECE + 1) // 2
    n_d2d = shard // PIECE

    @pl.when(source)
    def _():
        own_copy().wait()

        @pl.when(s == 1)
        def _():
            for u in range(own_steps - 1, split - 1, -1):
                z_down(u).start()

        first = jnp.where(s == 1, 0, own_steps)
        for i in range(own_steps):
            for m in (2 * i, 2 * i + 1):
                if m < n_d2d:
                    at = al(jnp.where(c == 0, plane - PIECE * (m + 1), PIECE * m), PIECE)
                    r = W.at[pl.ds(al(my_base + at, PIECE), PIECE)]
                    pltpu.make_async_remote_copy(
                        r, r, s_d2d_s.at[m], s_d2d_r.at[m],
                        device_id=(y, sib, x), device_id_type=MESH,
                    ).wait_recv()
            z_up(first + i).start()

        @pl.when(s == 1)
        def _():
            for u in range(split - 1, -1, -1):
                z_down(u).start()

    for slot in range(4):
        tap_local(slot).wait()
    for k in range(2):
        TF[k] = jnp.concatenate(
            [T[2 * k], T[2 * k + 1]], axis=1
        )
    cot_local.wait()
    cot_sib(1 - c).wait_recv()

    col = lax.broadcasted_iota(jnp.int32, (H.shape[3], LANES), 0)
    cols = H.shape[3]

    def before(a):
        return jnp.where(col == 0, 0.0, pltpu.roll(a, 1, 0))

    def after(a):
        return jnp.where(col == cols - 1, 0.0, pltpu.roll(a, cols - 1, 0))

    def needed(u):
        return jnp.logical_or(
            s >= 2,
            jnp.logical_or(
                jnp.logical_and(s == 0, u < own_steps), jnp.logical_and(s == 1, u >= own_steps)
            ),
        )

    def u_of(i):
        return jnp.where(s == 0, steps - 1 - i, i)

    def take(j):
        for h in range(2):
            u = u_of(2 * j + h)

            @pl.when(needed(u))
            def _():
                z_up(u).wait_recv()

                @pl.when(jnp.logical_or(s == 1, s == 2))
                def _():
                    z_up(u).start()

                y_copy(u, y).start()

    def halo_in(g):
        for k in range(2):
            hid_local(g, k).wait()
            hid_sib(g, k, False).wait_recv()
            for img in range(2):
                hid_x_recv(img, g, k).wait_recv()

    def stage_a(j):
        b = block_of(j)
        lane = pl.ds(al(b * LANES, LANES), LANES)
        for h in range(2):
            u = u_of(2 * j + h)

            @pl.when(needed(u))
            def _():
                y_copy(u, 1 - y).wait_recv()

        wb = W[lane, :]
        ext = {}
        tf = [TF[k, :, lane] for k in range(2)]
        sums = [[None] * 10, [None] * 10]
        for img in range(2):
            dg = lax.dot_general(
                C[img], wb, (((1,), (1,)), ((), ())), preferred_element_type=F32
            )
            pre = [[], []]
            rows = [None, None]
            for k in range(2):
                hal = HH[k, img, :, lane].astype(F32)
                rows[k] = [
                    jnp.where(x == 1, hal, 0.0),
                    H[k, img, 0, :, lane].astype(F32),
                    H[k, img, 1, :, lane].astype(F32),
                    jnp.where(x == 0, hal, 0.0),
                ]
                for r in range(2):
                    a = [
                        sum(tf[k][3 * i + jj : 3 * i + jj + 1] * rows[k][r + i] for i in range(3))
                        for jj in range(3)
                    ]
                    pre[k].append(before(a[0]) + (a[1] + tf[k][9:10]) + after(a[2]))
            for r in range(2):
                v, gt = pre[0][r], pre[1][r]
                sg = jax.nn.sigmoid(gt)
                si = gt * sg
                at = img * 2 * cols + r * cols
                GLU[at : at + cols, lane] = (v * si).astype(BF16)
                d = dg[r * cols : (r + 1) * cols]
                dv = (d * si).astype(BF16)
                dq = (d * v * (sg * (1.0 + gt * (1.0 - sg)))).astype(BF16)
                D[b, r, 0, img] = dv
                D[b, r, 1, img] = dq
                for k, dd in ((0, dv), (1, dq)):
                    dd = dd.astype(F32)
                    shifted = (after(dd), dd, before(dd))
                    for i in range(3):
                        for jj in range(3):
                            t = rows[k][r + i] * shifted[jj]
                            n = 3 * i + jj
                            sums[k][n] = t if sums[k][n] is None else sums[k][n] + t
                    sums[k][9] = dd if sums[k][9] is None else sums[k][9] + dd
        d_halo(b, 1 - x).start()
        for k in range(2):
            for n in range(10):
                G[k, n : n + 1, lane] = jnp.sum(sums[k][n], axis=0, keepdims=True)

    def out_lanes(b, k):
        return pl.ds(al(k * hidden_units + c * half + b * LANES, LANES), LANES)

    def o_local(b, k):
        lane = pl.ds(al(b * LANES, LANES), LANES)
        return pltpu.make_async_copy(
            DHS.at[k, c, :, :, lane], dhid.at[0, :, :, out_lanes(b, k)], s_ol.at[b, k]
        )

    def o_sib(b, k):
        lane = pl.ds(al(b * LANES, LANES), LANES)
        return pltpu.make_async_remote_copy(
            DHS.at[k, 1 - c, :, :, lane], dhid.at[0, :, :, out_lanes(b, k)],
            s_os.at[b, k], s_or.at[b, k], device_id=(y, sib, x), device_id_type=MESH,
        )

    def o_sib_in(b, k):
        lane = pl.ds(al(b * LANES, LANES), LANES)
        return pltpu.make_async_remote_copy(
            DHS.at[k, c, :, :, lane],
            dhid.at[0, :, :, pl.ds(al(k * hidden_units + (1 - c) * half + b * LANES, LANES), LANES)],
            s_os.at[b, k], s_or.at[b, k], device_id=(y, sib, x), device_id_type=MESH,
        )

    def stage_b(j):
        b = block_of(j)
        lane = pl.ds(al(b * LANES, LANES), LANES)
        d_halo(b, 1 - x).wait_recv()
        for k in range(2):
            tf = TF[k, :, lane]
            for img in range(2):
                hal = DH[b, k, img].astype(F32)
                rows = [
                    jnp.where(x == 1, hal, 0.0),
                    D[b, 0, k, img].astype(F32),
                    D[b, 1, k, img].astype(F32),
                    jnp.where(x == 0, hal, 0.0),
                ]
                for r in range(2):
                    a = [
                        sum(tf[3 * i + jj : 3 * i + jj + 1] * rows[r + 2 - i] for i in range(3))
                        for jj in range(3)
                    ]
                    DHS[k, img, r, :, lane] = (after(a[0]) + a[1] + before(a[2])).astype(BF16)
            o_local(b, k).start()
            o_sib(b, k).start()

    for first_j in range(AHEAD):
        take(first_j)

    @pl.loop(0, blocks)
    def _(j):
        for g in range(len(groups)):
            @pl.when(j == groups[g][0])
            def _():
                halo_in(g)

        @pl.when(j < blocks - AHEAD)
        def _():
            take(j + AHEAD)

        stage_a(j)

        @pl.when(j >= 2)
        def _():
            stage_b(j - 2)

    for k in range(2):
        GS[2 * k] = G[k, :, 0:plane]
        GS[2 * k + 1] = G[k, :, plane:]

    my_slot = 2 * z + x

    def g_dev(n, xx):
        return 2 * (2 * (n // 2) + c) + (n % 2)

    def g_send(n, xx):
        return pltpu.make_async_remote_copy(
            GS.at[n], R.at[my_slot], s_gs.at[n, xx], s_gr.at[my_slot],
            device_id=(y, g_dev(n, xx), xx), device_id_type=MESH,
        )

    def g_self(n, xx):
        return jnp.logical_and(g_dev(n, xx) == f, x == xx)

    for n in range(4):
        for xx in range(2):
            @pl.when(g_self(n, xx))
            def _():
                pltpu.make_async_copy(GS.at[n], R.at[my_slot], s_gr.at[my_slot]).start()

            @pl.when(jnp.logical_not(g_self(n, xx)))
            def _():
                g_send(n, xx).start()

    tokens = 2 * cols
    part = []
    n_at = 0
    while n_at < features:
        part.append((n_at, min(512, features - n_at)))
        n_at += 512

    def product(img, at, n):
        g = GLU[pl.ds(al(img * tokens, tokens), tokens), :]
        return jnp.dot(g, W[:, at : at + n], preferred_element_type=F32)

    for at, n in part:
        PS[:, at : at + n] = product(1 - c, at, n).astype(BF16)
    p_copy = pltpu.make_async_remote_copy(
        PS, PR, s_ps, s_pr, device_id=(y, sib, x), device_id_type=MESH
    )
    p_copy.start()
    stage_b(blocks - 2)
    stage_b(blocks - 1)
    mine = [product(c, at, n) for at, n in part]
    p_copy.wait_recv()
    for (at, n), m in zip(part, mine):
        out[:, at : at + n] = (m + PR[:, at : at + n].astype(F32)).astype(BF16)

    for slot in range(8):
        pltpu.make_async_copy(GS.at[0], R.at[slot], s_gr.at[slot]).wait()
    total = R[0]
    for slot in range(1, 8):
        total = total + R[slot]
    tgrad[...] = total[0:9]
    bgrad[...] = total[9:10]

    for n in range(4):
        for xx in range(2):
            @pl.when(jnp.logical_not(g_self(n, xx)))
            def _():
                g_send(n, xx).wait_send()
    p_copy.wait_send()
    for zz in range(4):
        @pl.when(jnp.logical_or(jnp.logical_not(is_self), z != zz))
        def _():
            tap_send(zz).wait_send()

    @pl.when(jnp.logical_not(source))
    def _():
        for k in range(n_d2d):
            d2d(k).wait_send()

    cot_sib(c).wait_send()
    for g in range(len(groups)):
        for k in range(2):
            for core in range(2):
                hid_x_send(core, g, k).wait_send()
            hid_sib(g, k, True).wait_send()

    @pl.loop(0, steps)
    def _(u):
        @pl.when(jnp.logical_or(s == 1, jnp.logical_or(s == 2, jnp.logical_and(s == 0, u >= own_steps))))
        def _():
            z_up(u).wait_send()

        @pl.when(jnp.logical_and(s == 1, u < own_steps))
        def _():
            z_down(u).wait_send()

        @pl.when(needed(u))
        def _():
            y_copy(u, y).wait_send()

    @pl.loop(0, blocks)
    def _(b):
        d_halo(b, 1 - x).wait_send()
        for k in range(2):
            o_local(b, k).wait()
            o_sib(b, k).wait_send()
            o_sib_in(b, k).wait_recv()


def fused_body(hidden_in, tap_weights, tap_bias, w_out, cotangent):
    _, rows, cols, channels = hidden_in.shape
    shard, features = w_out.shape
    own_channels = tap_weights.shape[1]
    half = channels // 4
    blocks = half // LANES
    tokens = rows * cols
    steps = half // (2 * PIECE)
    n_groups = len(halo_groups(blocks))
    dma = pltpu.SemaphoreType.DMA
    flops = 2 * 2 * 2 * tokens * half * features
    out, d_hidden, tgrad, bgrad = pl.pallas_call(
        unit_kernel,
        out_shape=(
            jax.ShapeDtypeStruct((tokens, features), BF16),
            jax.ShapeDtypeStruct(hidden_in.shape, BF16),
            jax.ShapeDtypeStruct((9, own_channels), F32),
            jax.ShapeDtypeStruct((1, own_channels), F32),
        ),
        in_specs=[
            pl.BlockSpec(memory_space=pl.ANY),
            pl.BlockSpec(memory_space=pltpu.VMEM),
            pl.BlockSpec(memory_space=pltpu.VMEM),
            pl.BlockSpec(memory_space=pl.ANY),
            pl.BlockSpec(memory_space=pl.ANY),
        ],
        out_specs=(
            pl.BlockSpec(memory_space=pltpu.VMEM),
            pl.BlockSpec(memory_space=pl.ANY),
            pl.BlockSpec(memory_space=pltpu.VMEM),
            pl.BlockSpec(memory_space=pltpu.VMEM),
        ),
        scratch_shapes=[
            pltpu.VMEM((half, features), BF16),
            pltpu.VMEM((2, tokens, features), BF16),
            pltpu.VMEM((2, 2, rows, cols, half), BF16),
            pltpu.VMEM((2, 2, cols, half), BF16),
            pltpu.VMEM((4, 16, own_channels), F32),
            pltpu.VMEM((2, 16, half), F32),
            pltpu.VMEM((2 * tokens, half), BF16),
            pltpu.VMEM((blocks, rows, 2, 2, cols, LANES), BF16),
            pltpu.VMEM((blocks, 2, 2, cols, LANES), BF16),
            pltpu.VMEM((2, 2, rows, cols, half), BF16),
            pltpu.VMEM((2, 16, half), F32),
            pltpu.VMEM((4, 16, own_channels), F32),
            pltpu.VMEM((8, 16, own_channels), F32),
            pltpu.VMEM((tokens, features), BF16),
            pltpu.VMEM((tokens, features), BF16),
            pltpu.VMEM((16, own_channels), F32),
            dma, dma((3,)), dma((shard // PIECE,)), dma((shard // PIECE,)),
            dma((steps,)), dma((steps // 2,)), dma((steps,)), dma((steps,)), dma((steps,)),
            dma((n_groups, 2)), dma((n_groups, 2)), dma((n_groups, 2)),
            dma((2, n_groups, 2)), dma((2, n_groups, 2)),
            dma((4,)), dma((4,)), dma((blocks,)), dma((blocks,)),
            dma((blocks, 2)), dma((blocks, 2)), dma((blocks, 2)),
            dma((4, 2)), dma((8,)), dma, dma,
        ],
        compiler_params=pltpu.CompilerParams(
            collective_id=0, has_side_effects=True, vmem_limit_bytes=56 * 1024 * 1024
        ),
        cost_estimate=pl.CostEstimate(flops=flops, bytes_accessed=8 << 20, transcendentals=0),
    )(hidden_in, tap_weights, tap_bias.reshape(1, own_channels), w_out, cotangent.reshape(tokens, features))
    return (
        out.reshape(cotangent.shape), d_hidden, tgrad, bgrad.reshape(own_channels),
    )


def fits(mesh, hidden_in, tap_weights, tap_bias, w_out, cotangent):
    if (mesh.shape["groups"], mesh.shape["fsdp"], mesh.shape["band"]) != (2, 8, 2):
        return False
    images, rows, cols, channels = hidden_in.shape
    return (
        images == 1
        and rows == 2
        and cols % 16 == 0
        and (channels // 4) % (2 * LANES) == LANES
        and w_out.shape[0] % PIECE == 0
        and (w_out.shape[0] // PIECE) % 2 == 1
        and 4 * w_out.shape[0] == channels // 4
        and 8 * tap_weights.shape[1] == channels
    )


def body(mesh, *args):
    if fits(mesh, *args):
        return fused_body(*args)
    return general_body(*args)


def solution(mesh):
    placed = (
        P(("groups", "fsdp"), "band", None, None),
        P(None, "fsdp"),
        P("fsdp"),
        P("fsdp", None),
        P(("groups", "fsdp"), "band", None, None),
    )
    return jax.shard_map(
        functools.partial(body, mesh),
        mesh=mesh,
        in_specs=placed,
        out_specs=(
            P(("groups", "fsdp"), "band", None, None),
            P(("groups", "fsdp"), "band", None, None),
            P("groups", "fsdp"),
            P(("groups", "fsdp")),
        ),
        check_vma=False,
    )
```
